256 devices in a mesh: outer: 32 (over y, x, core), inner: 8 (over z).
Axes of the slice: x: 4, y: 4, z: 8, core: 2. Of those that a mesh axis runs over, the one named last changes fastest.
Arguments:
- query_matrix: bfloat16 [32768, 8192], P(('outer', 'inner')), may hold values from -400 to 400
- key_matrix: bfloat16 [32768, 1024], P(('outer', 'inner')), may hold values from -6 to 6
- value_matrix: bfloat16 [32768, 1024], P(('outer', 'inner')), may hold values from -6 to 6
- output_gradient: bfloat16 [32768, 8192], P(('outer', 'inner')), may hold values from -6 to 6
- doc_ids: int32 [32768], replicated, may hold values from 0 to 127, never falling along the last dimension, each value on 1 to 512 neighbouring positions
Outputs:
- attended: bfloat16 [32768, 8192], P(('outer', 'inner'))
- query_grad: bfloat16 [32768, 8192], P(('outer', 'inner'))
- key_grad: bfloat16 [32768, 1024], P(('outer', 'inner'))
- value_grad: bfloat16 [32768, 1024], P(('outer', 'inner'))
The draws below stay inside these ranges and needn't reach their ends.
Inputs may be any that keep to these rules, and one draw needn't show every extreme that they name: `doc_ids`: each token's document number; it never falls along the sequence, and a document holds 1 to 512 tokens.
All inputs are finite; a program needn't handle non-finite values.
Results may differ from the reference program's by a relative error of at most 0.039.
Values may be sent and summed in bfloat16 or wider, within the bound.
A program may use at most 128 MiB of HBM per device.

```python
import math
import jax
import jax.numpy as jnp
import numpy as np
from jax import lax

QUERY_HEADS = 64
KEY_VALUE_HEADS = 8
HEAD_SIZE = 128
BLOCK_TOKENS = 128
PACKED_TOKENS = 32768
DOCS = 128


def drawn_pair(key):
    base_key = jax.random.fold_in(key, 7)
    flowing_parts = jax.random.split(base_key, 2)
    key_random_sample = jnp.clip(jax.random.normal(flowing_parts[0], (PACKED_TOKENS, KEY_VALUE_HEADS * HEAD_SIZE), jnp.float32), -6.0, 6.0)
    query_draw = jnp.clip(jax.random.normal(flowing_parts[1], (PACKED_TOKENS, QUERY_HEADS * HEAD_SIZE), jnp.float32), -6.0, 6.0)
    return (query_draw, key_random_sample)


def draw_query_matrix(key, part):
    return drawn_pair(key)[0].astype(jnp.bfloat16)


def draw_key_matrix(key, part):
    return drawn_pair(key)[1].astype(jnp.bfloat16)


def block_scale(rng, shape, pieces, smallest, top_value):
    level, own = 1.0, jax.random.fold_in(rng, 6)
    for position, shards_of in pieces:
        steps = jnp.exp(jax.random.uniform(jax.random.fold_in(own, position), (shards_of,), jnp.float32, smallest / len(pieces), top_value / len(pieces)))
        level = level * jnp.repeat(steps, shape[position] // shards_of).reshape([-1 if axis == position else 1 for axis in range(len(shape))])
    return level


def length_profile(amount, total, reach, skew):
    portions = [(1 << 20) // math.isqrt(standing ** skew) + 1 for standing in range(2, amount + 1)]
    surplus, counts = total - reach - (amount - 1), [1] * (amount - 1)
    while surplus > 0:
        candidates = [i for i in range(amount - 1) if counts[i] < reach]
        whole, left = sum([portions[i] for i in candidates]), surplus
        for i in candidates:
            addition = min(reach - counts[i], max(1, left * portions[i] // whole), surplus)
            counts[i] = counts[i] + addition
            surplus = surplus - addition
    return np.array([reach] + counts)


def ragged(rng, amount, total, most, slope):
    if amount == 2:
        one = jax.random.randint(rng, (), max(1, total - most), min(most, total - 1) + 1)
        return jnp.stack([one, total - one])
    sizes = jnp.asarray(length_profile(amount, total, most, slope), jnp.int32)
    couples = (amount - 1) // 2
    giver, receiver = sizes[1:1 + 2 * couples:2], sizes[2:2 + 2 * couples:2]
    slack = jnp.minimum(giver - 1, most - receiver)
    passed = jax.random.randint(jax.random.fold_in(rng, 1), (couples,), 0, 1 << 20) % (slack + 1)
    sizes = sizes.at[1:1 + 2 * couples:2].set(giver - passed).at[2:2 + 2 * couples:2].set(receiver + passed)
    return sizes[jax.random.permutation(jax.random.fold_in(rng, 2), amount)]


def gaussian(own_key, shape, scale, bound, pieces=(), kind=jnp.bfloat16):
    values = jax.random.normal(own_key, shape, jnp.float32) * scale
    if len(pieces) > 0:
        values = block_scale(own_key, shape, pieces, -0.22, 0.18) * values
    return jnp.clip(values, min=-bound, max=bound).astype(kind)


def setup_inputs(seed: int = 0) -> dict:
    key_list = jax.random.split(jax.random.key(seed), 6)
    return {
        "query_matrix": draw_query_matrix(jax.random.fold_in(key_list[5], 71), 0),
        "key_matrix": draw_key_matrix(jax.random.fold_in(key_list[5], 71), 0),
        "value_matrix": gaussian(key_list[2], (PACKED_TOKENS, KEY_VALUE_HEADS * HEAD_SIZE), 1.0, 6.0, ((0, 256),)),
        "output_gradient": gaussian(key_list[3], (PACKED_TOKENS, QUERY_HEADS * HEAD_SIZE), 1.0, 6.0, ((0, 256),)),
        "doc_ids": jnp.searchsorted(jnp.cumsum(ragged(key_list[4], DOCS, PACKED_TOKENS, 4 * BLOCK_TOKENS, 2)), jnp.arange(PACKED_TOKENS), side="right").astype(jnp.int32),
    }


NEG = -1e30


def reference(query_matrix, key_matrix, value_matrix, output_gradient, doc_ids):
    heads_per_group = QUERY_HEADS // KEY_VALUE_HEADS
    block_total = PACKED_TOKENS // BLOCK_TOKENS
    scaling = HEAD_SIZE ** -0.5
    padded_keys = jnp.concatenate([jnp.zeros((2 * BLOCK_TOKENS, KEY_VALUE_HEADS * HEAD_SIZE), key_matrix.dtype), key_matrix]).reshape(PACKED_TOKENS + 2 * BLOCK_TOKENS, KEY_VALUE_HEADS, HEAD_SIZE)
    padded_values = jnp.concatenate([jnp.zeros((2 * BLOCK_TOKENS, KEY_VALUE_HEADS * HEAD_SIZE), value_matrix.dtype), value_matrix]).reshape(PACKED_TOKENS + 2 * BLOCK_TOKENS, KEY_VALUE_HEADS, HEAD_SIZE)
    pad_labels = jnp.concatenate([jnp.full((2 * BLOCK_TOKENS,), -1, jnp.int32), doc_ids.astype(jnp.int32)])

    def per_block(running, block_id):
        key_running_sum, value_running_sum = running
        starting_row = (block_id * BLOCK_TOKENS).astype(jnp.int32)
        query_matrix_list = lax.dynamic_slice_in_dim(query_matrix, starting_row, BLOCK_TOKENS).reshape(BLOCK_TOKENS, KEY_VALUE_HEADS, heads_per_group, HEAD_SIZE).astype(jnp.float32)
        window_gradient = lax.dynamic_slice_in_dim(output_gradient, starting_row, BLOCK_TOKENS).reshape(BLOCK_TOKENS, KEY_VALUE_HEADS, heads_per_group, HEAD_SIZE).astype(jnp.float32)
        key_win = lax.dynamic_slice_in_dim(padded_keys, starting_row, 3 * BLOCK_TOKENS).astype(jnp.float32)
        value_win = lax.dynamic_slice_in_dim(padded_values, starting_row, 3 * BLOCK_TOKENS).astype(jnp.float32)
        query_labels = lax.dynamic_slice_in_dim(doc_ids.astype(jnp.int32), starting_row, BLOCK_TOKENS)
        key_labels = lax.dynamic_slice_in_dim(pad_labels, starting_row, 3 * BLOCK_TOKENS)
        query_places = starting_row + jnp.arange(BLOCK_TOKENS, dtype=jnp.int32)
        key_places = starting_row - 2 * BLOCK_TOKENS + jnp.arange(3 * BLOCK_TOKENS, dtype=jnp.int32)
        allowed = (query_labels[:, None] == key_labels[None, :]) & (key_places[None, :] <= query_places[:, None])
        raw_scores = jnp.einsum("tkgd,ckd->kgtc", query_matrix_list, key_win) * scaling
        scores = jnp.where(allowed, raw_scores, NEG)
        row_top = jnp.max(scores, axis=-1)
        weights = jnp.where(allowed, jnp.exp(scores - row_top[..., None]), 0.0)
        row_total = jnp.sum(weights, axis=-1)
        coarse = lax.optimization_barrier(weights.astype(jnp.bfloat16)).astype(jnp.float32)
        summed = jnp.einsum("kgtc,ckd->tkgd", coarse, value_win)
        attended = (summed / jnp.transpose(row_total, (2, 0, 1))[..., None]).astype(jnp.bfloat16)
        log_total = row_top + jnp.log(row_total)
        row_dot = jnp.transpose(jnp.sum(window_gradient * attended.astype(jnp.float32), axis=-1), (1, 2, 0))
        probs = jnp.where(allowed, jnp.exp(raw_scores - log_total[..., None]), 0.0)
        grad_weights = jnp.einsum("tkgd,ckd->kgtc", window_gradient, value_win)
        grad_scores = probs * (grad_weights - row_dot[..., None])
        grad_coarse = lax.optimization_barrier(grad_scores.astype(jnp.bfloat16)).astype(jnp.float32)
        prob_coarse = lax.optimization_barrier(probs.astype(jnp.bfloat16)).astype(jnp.float32)
        query_part = jnp.einsum("kgtc,ckd->tkgd", grad_coarse, key_win) * scaling
        key_portion = jnp.einsum("kgtc,tkgd->ckd", grad_coarse, query_matrix_list) * scaling
        value_portion = jnp.einsum("kgtc,tkgd->ckd", prob_coarse, window_gradient)
        key_running_sum = lax.dynamic_update_slice_in_dim(key_running_sum, lax.dynamic_slice_in_dim(key_running_sum, starting_row, 3 * BLOCK_TOKENS) + key_portion.reshape(3 * BLOCK_TOKENS, KEY_VALUE_HEADS * HEAD_SIZE), starting_row, 0)
        value_running_sum = lax.dynamic_update_slice_in_dim(value_running_sum, lax.dynamic_slice_in_dim(value_running_sum, starting_row, 3 * BLOCK_TOKENS) + value_portion.reshape(3 * BLOCK_TOKENS, KEY_VALUE_HEADS * HEAD_SIZE), starting_row, 0)
        return (key_running_sum, value_running_sum), (attended.reshape(BLOCK_TOKENS, QUERY_HEADS * HEAD_SIZE), query_part.reshape(BLOCK_TOKENS, QUERY_HEADS * HEAD_SIZE).astype(jnp.bfloat16))

    starting_carry = (jnp.zeros((PACKED_TOKENS + 2 * BLOCK_TOKENS, KEY_VALUE_HEADS * HEAD_SIZE), jnp.float32), jnp.zeros((PACKED_TOKENS + 2 * BLOCK_TOKENS, KEY_VALUE_HEADS * HEAD_SIZE), jnp.float32))
    (key_running_sum, value_running_sum), (attended, query_grad) = lax.scan(per_block, starting_carry, jnp.arange(block_total, dtype=jnp.int32))
    return (attended.reshape(PACKED_TOKENS, QUERY_HEADS * HEAD_SIZE), query_grad.reshape(PACKED_TOKENS, QUERY_HEADS * HEAD_SIZE), key_running_sum[2 * BLOCK_TOKENS:].astype(jnp.bfloat16), value_running_sum[2 * BLOCK_TOKENS:].astype(jnp.bfloat16))
```

```python
import functools

import jax
import jax.numpy as jnp
from jax import lax
from jax.experimental import pallas as pl
from jax.experimental.pallas import tpu as pltpu
from jax.sharding import PartitionSpec as P

KEY_VALUE_HEADS = 8
GROUP = 8
HEAD_SIZE = 128
BLOCK = 128
WIDE = GROUP * HEAD_SIZE
NEG = -1e30
SCALING = HEAD_SIZE**-0.5
LOG2E = 1.4426950408889634
PAIR = 2
AHEAD = 3
MESH = pl.DeviceIdType.MESH

NT = (((1,), (1,)), ((), ()))


def dot(a, b):
    return jnp.dot(a, b, preferred_element_type=jnp.float32)


def columns(head, width):
    return pl.ds(pl.multiple_of(head * width, width), width)


def kernel(
    outer_count,
    inner_count,
    q_hbm,
    k_hbm,
    v_hbm,
    g_hbm,
    doc_hbm,
    att_hbm,
    dq_hbm,
    dk_hbm,
    dv_hbm,
    q,
    g,
    docs,
    bias,
    kv,
    part,
    far_out,
    far_in,
    sum_out,
    sum_in,
    att,
    dq,
    dkv,
    in_sem,
    own_sem,
    doc_sem,
    own_send,
    near_recv,
    fwd_send,
    far_recv,
    back_send,
    back_recv,
    sum_send,
    sum_recv,
    out_sem,
    dkv_sem,
):
    place = lax.axis_index("outer") * inner_count + lax.axis_index("inner")
    total = outer_count * inner_count
    after = lax.rem(place + 1, total)
    before = lax.rem(place + total - 1, total)
    next_id = (after // inner_count, lax.rem(after, inner_count))
    prev_id = (before // inner_count, lax.rem(before, inner_count))

    def remote(src, dst, send, recv, device):
        return pltpu.make_async_remote_copy(
            src_ref=src,
            dst_ref=dst,
            send_sem=send,
            recv_sem=recv,
            device_id=device,
            device_id_type=MESH,
        )

    def own_copy(h, which):
        source = (k_hbm, v_hbm)[which]
        return remote(
            source.at[:, columns(h, HEAD_SIZE)],
            kv.at[h, which, 1],
            own_send.at[h, which],
            near_recv.at[h, which],
            next_id,
        )

    def forward_copy(h):
        return remote(kv.at[h, :, 1], kv.at[h, :, 2], fwd_send.at[h], far_recv.at[h], next_id)

    def back_copy(h, which):
        return remote(
            far_out.at[h, which],
            far_in.at[h, which],
            back_send.at[h, which],
            back_recv.at[h, which],
            prev_id,
        )

    def sum_copy(h):
        return remote(sum_out.at[h], sum_in.at[h], sum_send.at[h], sum_recv.at[h], prev_id)

    def load_copies(h):
        wide = columns(h, WIDE)
        narrow = columns(h, HEAD_SIZE)
        return (
            pltpu.make_async_copy(q_hbm.at[:, wide], q.at[:, wide], in_sem.at[h, 0]),
            pltpu.make_async_copy(g_hbm.at[:, wide], g.at[:, wide], in_sem.at[h, 1]),
            pltpu.make_async_copy(k_hbm.at[:, narrow], kv.at[h, 0, 0], own_sem.at[h, 0]),
            pltpu.make_async_copy(v_hbm.at[:, narrow], kv.at[h, 1, 0], own_sem.at[h, 1]),
        )

    def store_copies(h):
        wide = columns(h, WIDE)
        return (
            pltpu.make_async_copy(att.at[:, wide], att_hbm.at[:, wide], out_sem.at[h, 0]),
            pltpu.make_async_copy(dq.at[:, wide], dq_hbm.at[:, wide], out_sem.at[h, 1]),
        )

    def grad_copies(h):
        narrow = columns(h, HEAD_SIZE)
        return (
            pltpu.make_async_copy(dkv.at[h, 0], dk_hbm.at[:, narrow], dkv_sem.at[h, 0]),
            pltpu.make_async_copy(dkv.at[h, 1], dv_hbm.at[:, narrow], dkv_sem.at[h, 1]),
        )

    doc_copy = pltpu.make_async_copy(doc_hbm, docs, doc_sem)
    doc_copy.start()

    barrier = pltpu.get_barrier_semaphore()
    for neighbour in (prev_id, next_id):
        pl.semaphore_signal(barrier, inc=1, device_id=neighbour, device_id_type=MESH)
    pl.semaphore_wait(barrier, 2)

    for h in range(AHEAD):
        own_copy(h, 0).start()
        own_copy(h, 1).start()

    def start_loads(h, carry):
        for copy in load_copies(h):
            copy.start()
        return carry

    lax.fori_loop(0, KEY_VALUE_HEADS, start_loads, 0)

    doc_copy.wait()
    own_labels = docs[pl.ds(place, 1), :]
    query_labels = jnp.broadcast_to(own_labels, (BLOCK, BLOCK))
    for which in range(3):
        row = docs[pl.ds(jnp.maximum(place - which, 0), 1), :]
        key_labels = jnp.broadcast_to(row, (BLOCK, BLOCK)).T
        allowed = key_labels == query_labels
        if which == 0:
            key_place = lax.broadcasted_iota(jnp.int32, (BLOCK, BLOCK), 0)
            query_place = lax.broadcasted_iota(jnp.int32, (BLOCK, BLOCK), 1)
            allowed = allowed & (key_place <= query_place)
        else:
            allowed = allowed & jnp.broadcast_to(place >= which, (BLOCK, BLOCK))
        bias[pl.ds(which * BLOCK, BLOCK), :] = jnp.where(allowed, 0.0, NEG)

    def pass_on(h):
        own_copy(h, 0).wait_recv()
        own_copy(h, 1).wait_recv()
        forward_copy(h).start()

    def combine(h):
        back_copy(h, 0).wait_recv()
        back_copy(h, 1).wait_recv()
        sum_out[h] = (part[h, :, 1] + far_in[h].astype(jnp.float32)).astype(jnp.bfloat16)
        sum_copy(h).start()

    def finish(h):
        sum_copy(h).wait_recv()
        dkv[h] = (part[h, :, 0] + sum_in[h].astype(jnp.float32)).astype(jnp.bfloat16)
        for copy in grad_copies(h):
            copy.start()

    def attend(h):
        keys = kv[h, 0].reshape(3 * BLOCK, HEAD_SIZE)
        values = kv[h, 1].reshape(3 * BLOCK, HEAD_SIZE)
        keys_t = keys.T
        values_t = values.T
        masked = bias[...]
        masked = jnp.concatenate([masked] * PAIR, axis=1)
        queries, grads, probs_all, scores_all = [], [], [], []
        for group in range(0, GROUP, PAIR):

            def rows(ref):
                return jnp.concatenate(
                    [ref[:, columns(h * GROUP + group + n, HEAD_SIZE)] for n in range(PAIR)],
                    axis=0,
                )

            query, grad = rows(q), rows(g)
            scores = lax.dot_general(keys, query, NT, preferred_element_type=jnp.float32)
            scores = scores * (SCALING * LOG2E) + masked
            top = jnp.max(scores, axis=0, keepdims=True)
            weights = jnp.exp2(scores - top)
            sums = jnp.sum(weights, axis=0, keepdims=True)
            probs = weights * (1.0 / sums)
            coarse = probs.astype(jnp.bfloat16)
            grad_weights = lax.dot_general(values, grad, NT, preferred_element_type=jnp.float32)
            products = probs * grad_weights
            row_dot = jnp.sum(products, axis=0, keepdims=True)
            grad_scores = (products - probs * row_dot).astype(jnp.bfloat16)
            attended = dot(values_t, coarse).astype(jnp.bfloat16)
            query_grad = (dot(keys_t, grad_scores) * SCALING).astype(jnp.bfloat16)
            for n in range(PAIR):
                place_of = columns(h * GROUP + group + n, HEAD_SIZE)
                att[:, place_of] = attended[:, n * BLOCK : (n + 1) * BLOCK].T
                dq[:, place_of] = query_grad[:, n * BLOCK : (n + 1) * BLOCK].T
            queries.append(query)
            grads.append(grad)
            probs_all.append(coarse)
            scores_all.append(grad_scores)
        grad_rows = jnp.concatenate(grads, axis=0)
        query_rows = jnp.concatenate(queries, axis=0)
        value_part = dot(jnp.concatenate(probs_all, axis=1), grad_rows)
        key_part = dot(jnp.concatenate(scores_all, axis=1), query_rows) * SCALING
        for which, value in ((0, key_part), (1, value_part)):
            far_out[h, which] = value[2 * BLOCK :].astype(jnp.bfloat16)
            part[h, which] = value[: 2 * BLOCK].reshape(2, BLOCK, HEAD_SIZE)
            back_copy(h, which).start()
        for copy in store_copies(h):
            copy.start()

    pass_on(0)

    def step(h, carry):
        @pl.when(h + 1 < KEY_VALUE_HEADS)
        def _():
            pass_on(h + 1)

        @pl.when(h + AHEAD < KEY_VALUE_HEADS)
        def _():
            own_copy(h + AHEAD, 0).start()
            own_copy(h + AHEAD, 1).start()

        for copy in load_copies(h):
            copy.wait()
        forward_copy(h).wait_recv()
        attend(h)

        @pl.when(h >= 1)
        def _():
            combine(h - 1)

        @pl.when(h >= 2)
        def _():
            finish(h - 2)

        return carry

    lax.fori_loop(0, KEY_VALUE_HEADS, step, 0)
    last = KEY_VALUE_HEADS - 1
    combine(last)
    finish(last - 1)
    finish(last)

    def drain(h, carry):
        own_copy(h, 0).wait_send()
        own_copy(h, 1).wait_send()
        forward_copy(h).wait_send()
        back_copy(h, 0).wait_send()
        back_copy(h, 1).wait_send()
        sum_copy(h).wait_send()
        for copy in store_copies(h):
            copy.wait()
        for copy in grad_copies(h):
            copy.wait()
        return carry

    lax.fori_loop(0, KEY_VALUE_HEADS, drain, 0)


def body(outer_count, inner_count, query_matrix, key_matrix, value_matrix, output_gradient, doc_ids):
    heads = KEY_VALUE_HEADS
    any_spec = pl.BlockSpec(memory_space=pl.ANY)
    labels = doc_ids.reshape(doc_ids.shape[0] // BLOCK, BLOCK)
    tile = (BLOCK, HEAD_SIZE)
    bf16, f32 = jnp.bfloat16, jnp.float32
    dma = pltpu.SemaphoreType.DMA
    return pl.pallas_call(
        functools.partial(kernel, outer_count, inner_count),
        out_shape=(
            jax.ShapeDtypeStruct(query_matrix.shape, bf16),
            jax.ShapeDtypeStruct(query_matrix.shape, bf16),
            jax.ShapeDtypeStruct(key_matrix.shape, bf16),
            jax.ShapeDtypeStruct(value_matrix.shape, bf16),
        ),
        in_specs=[any_spec] * 5,
        out_specs=(any_spec,) * 4,
        scratch_shapes=[
            pltpu.VMEM(query_matrix.shape, bf16),
            pltpu.VMEM(query_matrix.shape, bf16),
            pltpu.VMEM(labels.shape, jnp.int32),
            pltpu.VMEM((3 * BLOCK, BLOCK), f32),
            pltpu.VMEM((heads, 2, 3) + tile, bf16),
            pltpu.VMEM((heads, 2, 2) + tile, f32),
            pltpu.VMEM((heads, 2) + tile, bf16),
            pltpu.VMEM((heads, 2) + tile, bf16),
            pltpu.VMEM((heads, 2) + tile, bf16),
            pltpu.VMEM((heads, 2) + tile, bf16),
            pltpu.VMEM(query_matrix.shape, bf16),
            pltpu.VMEM(query_matrix.shape, bf16),
            pltpu.VMEM((heads, 2) + tile, bf16),
            dma((heads, 2)),
            dma((heads, 2)),
            dma(()),
            dma((heads, 2)),
            dma((heads, 2)),
            dma((heads,)),
            dma((heads,)),
            dma((heads, 2)),
            dma((heads, 2)),
            dma((heads,)),
            dma((heads,)),
            dma((heads, 2)),
            dma((heads, 2)),
        ],
        compiler_params=pltpu.CompilerParams(
            collective_id=0, has_side_effects=True, vmem_limit_bytes=48 * 1024 * 1024
        ),
    )(query_matrix, key_matrix, value_matrix, output_gradient, labels)


def solution(mesh):
    split = P(("outer", "inner"), None)
    return jax.shard_map(
        functools.partial(body, mesh.shape["outer"], mesh.shape["inner"]),
        mesh=mesh,
        in_specs=(split, split, split, split, P()),
        out_specs=(split, split, split, split),
        check_vma=False,
    )
```

```python
import functools

import jax
import jax.numpy as jnp
from jax import lax
from jax.experimental import pallas as pl
from jax.experimental.pallas import tpu as pltpu
from jax.sharding import PartitionSpec as P

HEADS = 8
GROUP = 8
HEAD_SIZE = 128
BLOCK = 128
WIDE = GROUP * HEAD_SIZE
NEG = -1e30
SCALING = HEAD_SIZE**-0.5
LOG2E = 1.4426950408889634
MESH = pl.DeviceIdType.MESH
BOTH = (0, 1)

NT = (((1,), (1,)), ((), ()))
TN = (((0,), (0,)), ((), ()))


def dot(a, b):
    return jnp.dot(a, b, preferred_element_type=jnp.float32)


def dot_of(a, b, dims):
    return lax.dot_general(a, b, dims, preferred_element_type=jnp.float32)


def columns(head, width):
    return pl.ds(pl.multiple_of(head * width, width), width)


def kernel(
    outer_count,
    inner_count,
    q_hbm,
    k_hbm,
    v_hbm,
    g_hbm,
    doc_hbm,
    att,
    dq,
    dk,
    dv,
    q,
    g,
    docs,
    bias,
    kv,
    part,
    far_out,
    far_in,
    sum_out,
    sum_in,
    in_sem,
    own_sem,
    doc_sem,
    own_send,
    near_recv,
    fwd_send,
    far_recv,
    back_send,
    back_recv,
    sum_send,
    sum_recv,
):
    place = lax.axis_index("outer") * inner_count + lax.axis_index("inner")
    total = outer_count * inner_count
    has_prev = place >= 1
    has_prev2 = place >= 2
    has_next = place <= total - 2
    has_both = has_prev & has_next
    after = jnp.minimum(place + 1, total - 1)
    before = jnp.maximum(place - 1, 0)
    next_id = (after // inner_count, lax.rem(after, inner_count))
    prev_id = (before // inner_count, lax.rem(before, inner_count))

    def remote(src, dst, send, recv, device):
        return pltpu.make_async_remote_copy(
            src_ref=src,
            dst_ref=dst,
            send_sem=send,
            recv_sem=recv,
            device_id=device,
            device_id_type=MESH,
        )

    def own_copy(h, which):
        source = (k_hbm, v_hbm)[which]
        return remote(
            source.at[:, columns(h, HEAD_SIZE)],
            kv.at[h, which, 1],
            own_send.at[h, which],
            near_recv.at[h, which],
            next_id,
        )

    def forward_copy(h, which):
        return remote(
            kv.at[h, which, 1],
            kv.at[h, which, 2],
            fwd_send.at[h, which],
            far_recv.at[h, which],
            next_id,
        )

    def back_copy(h, which):
        return remote(
            far_out.at[h, which],
            far_in.at[h, which],
            back_send.at[h, which],
            back_recv.at[h, which],
            prev_id,
        )

    def sum_copy(h, which):
        return remote(
            sum_out.at[h, which],
            sum_in.at[h, which],
            sum_send.at[h, which],
            sum_recv.at[h, which],
            prev_id,
        )

    def load_copies(h):
        wide = columns(h, WIDE)
        narrow = columns(h, HEAD_SIZE)
        return (
            pltpu.make_async_copy(q_hbm.at[:, wide], q.at[:, wide], in_sem.at[h, 0]),
            pltpu.make_async_copy(g_hbm.at[:, wide], g.at[:, wide], in_sem.at[h, 1]),
            pltpu.make_async_copy(k_hbm.at[:, narrow], kv.at[h, 0, 0], own_sem.at[h, 0]),
            pltpu.make_async_copy(v_hbm.at[:, narrow], kv.at[h, 1, 0], own_sem.at[h, 1]),
        )

    doc_copy = pltpu.make_async_copy(doc_hbm, docs, doc_sem)
    doc_copy.start()

    barrier = pltpu.get_barrier_semaphore()

    @pl.when(has_prev)
    def _():
        pl.semaphore_signal(barrier, inc=1, device_id=prev_id, device_id_type=MESH)

    @pl.when(has_next)
    def _():
        pl.semaphore_signal(barrier, inc=1, device_id=next_id, device_id_type=MESH)

    pl.semaphore_wait(barrier, jnp.where(has_both, 2, 1))

    def send_own(h):
        @pl.when(has_next)
        def _():
            for which in BOTH:
                own_copy(h, which).start()

    def pass_on(h):
        @pl.when(has_prev)
        def _():
            for which in BOTH:
                own_copy(h, which).wait_recv()

                @pl.when(has_next)
                def _():
                    forward_copy(h, which).start()

    send_own(0)
    send_own(1)

    def start_loads(h, carry):
        for copy in load_copies(h):
            copy.start()
        return carry

    lax.fori_loop(0, HEADS, start_loads, 0)

    @pl.when(place <= 1)
    def _():
        blank = jnp.zeros((HEADS, 2, BLOCK, HEAD_SIZE), jnp.bfloat16)
        kv[:, :, 2] = blank

        @pl.when(place == 0)
        def _():
            kv[:, :, 1] = blank

    @pl.when(place == total - 1)
    def _():
        far_in[...] = jnp.zeros_like(far_in)
        sum_in[...] = jnp.zeros_like(sum_in)

    doc_copy.wait()
    own_labels = jnp.broadcast_to(docs[pl.ds(place, 1), :], (BLOCK, BLOCK)).T
    for which in range(3):
        row = docs[pl.ds(jnp.maximum(place - which, 0), 1), :]
        allowed = jnp.broadcast_to(row, (BLOCK, BLOCK)) == own_labels
        if which == 0:
            query_place = lax.broadcasted_iota(jnp.int32, (BLOCK, BLOCK), 0)
            key_place = lax.broadcasted_iota(jnp.int32, (BLOCK, BLOCK), 1)
            allowed = allowed & (key_place <= query_place)
        else:
            allowed = allowed & jnp.broadcast_to(place >= which, (BLOCK, BLOCK))
        bias[:, which * BLOCK : (which + 1) * BLOCK] = jnp.where(allowed, 0.0, NEG)

    def combine(h):
        @pl.when(has_prev)
        def _():
            for which in (1, 0):

                @pl.when(has_next)
                def _():
                    back_copy(h, which).wait_recv()

                sum_out[h, which] = (
                    part[h, which, 1] + far_in[h, which].astype(jnp.float32)
                ).astype(jnp.bfloat16)
                sum_copy(h, which).start()

    def finish(h):
        for which in (1, 0):

            @pl.when(has_next)
            def _():
                sum_copy(h, which).wait_recv()

            (dk, dv)[which][:, columns(h, HEAD_SIZE)] = (
                part[h, which, 0] + sum_in[h, which].astype(jnp.float32)
            ).astype(jnp.bfloat16)

    def attend(h):
        keys = kv[h, 0].reshape(3 * BLOCK, HEAD_SIZE)
        values = kv[h, 1].reshape(3 * BLOCK, HEAD_SIZE)

        def rows(ref):
            return jnp.concatenate(
                [ref[:, columns(h * GROUP + n, HEAD_SIZE)] for n in range(GROUP)], axis=0
            )

        query, grad = rows(q), rows(g)
        scores = dot_of(query, keys, NT)
        grad_weights = dot_of(grad, values, NT)
        scores = scores * (SCALING * LOG2E) + jnp.concatenate([bias[...]] * GROUP, axis=0)
        top = jnp.max(scores, axis=1, keepdims=True)
        weights = jnp.exp2(scores - top)
        sums = jnp.sum(weights, axis=1, keepdims=True)
        probs = weights * (1.0 / sums)
        coarse = probs.astype(jnp.bfloat16)
        products = probs * grad_weights
        row_dot = jnp.sum(products, axis=1, keepdims=True)
        grad_scores = (products - probs * row_dot).astype(jnp.bfloat16)
        far_out[h, 1] = dot_of(coarse[:, 2 * BLOCK :], grad, TN).astype(jnp.bfloat16)
        far_out[h, 0] = (dot_of(grad_scores[:, 2 * BLOCK :], query, TN) * SCALING).astype(
            jnp.bfloat16
        )

        @pl.when(has_prev2)
        def _():
            for which in (1, 0):
                back_copy(h, which).start()

        value_part = dot_of(coarse[:, : 2 * BLOCK], grad, TN)
        key_part = dot_of(grad_scores[:, : 2 * BLOCK], query, TN) * SCALING
        for which, value in ((0, key_part), (1, value_part)):
            part[h, which] = value.reshape(2, BLOCK, HEAD_SIZE)
        attended = dot(coarse, values).astype(jnp.bfloat16)
        query_grad = (dot(grad_scores, keys) * SCALING).astype(jnp.bfloat16)
        for n in range(GROUP):
            place_of = columns(h * GROUP + n, HEAD_SIZE)
            att[:, place_of] = attended[n * BLOCK : (n + 1) * BLOCK]
            dq[:, place_of] = query_grad[n * BLOCK : (n + 1) * BLOCK]

    pass_on(0)
    send_own(2)
    pass_on(1)
    send_own(3)

    def step(h, carry):
        for copy in load_copies(h):
            copy.wait()

        @pl.when(has_prev2)
        def _():
            for which in BOTH:
                forward_copy(h, which).wait_recv()

        attend(h)

        @pl.when(h + 2 < HEADS)
        def _():
            pass_on(h + 2)

        @pl.when(h + 4 < HEADS)
        def _():
            send_own(h + 4)

        @pl.when(h >= 1)
        def _():
            combine(h - 1)

        @pl.when(h >= 3)
        def _():
            finish(h - 3)

        return carry

    lax.fori_loop(0, HEADS, step, 0)
    combine(HEADS - 1)
    for late in (3, 2, 1):
        finish(HEADS - late)

    def drain(h, carry):
        for which in BOTH:

            @pl.when(has_next)
            def _():
                own_copy(h, which).wait_send()

            @pl.when(has_both)
            def _():
                forward_copy(h, which).wait_send()

            @pl.when(has_prev2)
            def _():
                back_copy(h, which).wait_send()

            @pl.when(has_prev)
            def _():
                sum_copy(h, which).wait_send()

        return carry

    lax.fori_loop(0, HEADS, drain, 0)


def store_kernel(*refs):
    sources, targets, sems = refs[:4], refs[4:8], refs[8]
    copies = [
        pltpu.make_async_copy(source, target, sems.at[n])
        for n, (source, target) in enumerate(zip(sources, targets))
    ]
    for copy in copies:
        copy.start()
    for copy in copies:
        copy.wait()


def body(outer_count, inner_count, query_matrix, key_matrix, value_matrix, output_gradient, doc_ids):
    hbm = pl.BlockSpec(memory_space=pltpu.HBM)
    vmem = pl.BlockSpec(memory_space=pltpu.VMEM)
    labels = doc_ids.reshape(doc_ids.shape[0] // BLOCK, BLOCK)
    tile = (BLOCK, HEAD_SIZE)
    bf16, f32 = jnp.bfloat16, jnp.float32
    dma = pltpu.SemaphoreType.DMA
    shapes = [query_matrix.shape, query_matrix.shape, key_matrix.shape, value_matrix.shape]
    operands = [
        pltpu.with_memory_space_constraint(operand, pltpu.HBM)
        for operand in (query_matrix, key_matrix, value_matrix, output_gradient, labels)
    ]
    results = pl.pallas_call(
        functools.partial(kernel, outer_count, inner_count),
        out_shape=[pltpu.VMEM(shape, bf16) for shape in shapes],
        in_specs=[hbm] * 5,
        out_specs=[vmem] * 4,
        scratch_shapes=[
            pltpu.VMEM(query_matrix.shape, bf16),
            pltpu.VMEM(query_matrix.shape, bf16),
            pltpu.VMEM(labels.shape, jnp.int32),
            pltpu.VMEM((BLOCK, 3 * BLOCK), f32),
            pltpu.VMEM((HEADS, 2, 3) + tile, bf16),
            pltpu.VMEM((HEADS, 2, 2) + tile, f32),
        ]
        + [pltpu.VMEM((HEADS, 2) + tile, bf16)] * 4
        + [dma((HEADS, 2)), dma((HEADS, 2)), dma(())]
        + [dma((HEADS, 2))] * 8,
        compiler_params=pltpu.CompilerParams(
            collective_id=0, has_side_effects=True, vmem_limit_bytes=44 * 1024 * 1024
        ),
    )(*operands)
    results = [pltpu.with_memory_space_constraint(result, pltpu.VMEM) for result in results]
    return pl.pallas_call(
        store_kernel,
        out_shape=[jax.ShapeDtypeStruct(shape, bf16) for shape in shapes],
        in_specs=[vmem] * 4,
        out_specs=[pl.BlockSpec(memory_space=pltpu.HBM)] * 4,
        scratch_shapes=[dma((4,))],
        compiler_params=pltpu.CompilerParams(vmem_limit_bytes=1024 * 1024),
    )(*results)


def solution(mesh):
    split = P(("outer", "inner"), None)
    return jax.shard_map(
        functools.partial(body, mesh.shape["outer"], mesh.shape["inner"]),
        mesh=mesh,
        in_specs=(split, split, split, split, P()),
        out_specs=(split, split, split, split),
        check_vma=False,
    )
```

```python
import functools

import jax
import jax.numpy as jnp
from jax import lax
from jax.experimental import pallas as pl
from jax.experimental.pallas import tpu as pltpu
from jax.sharding import PartitionSpec as P

HEADS = 8
GROUP = 8
HEAD_SIZE = 128
BLOCK = 128
WIDE = GROUP * HEAD_SIZE
NEG = -1e30
SCALING = HEAD_SIZE**-0.5
LOG2E = 1.4426950408889634
MESH = pl.DeviceIdType.MESH
BOTH = (0, 1)
INIT = 2
LEAD = 2
LAG = 2
FINAL = 4
LOADS = 2
EXTRA = 2
EARLY = 1
SPLIT = 2

NT = (((1,), (1,)), ((), ()))
TN = (((0,), (0,)), ((), ()))


def dot(a, b):
    return jnp.dot(a, b, preferred_element_type=jnp.float32)


def dot_of(a, b, dims):
    return lax.dot_general(a, b, dims, preferred_element_type=jnp.float32)


def columns(head, width):
    return pl.ds(pl.multiple_of(head * width, width), width)


def kernel(
    outer_count,
    inner_count,
    q_hbm,
    k_hbm,
    v_hbm,
    g_hbm,
    doc_hbm,
    att,
    dq,
    dk,
    dv,
    q,
    g,
    docs,
    bias,
    kv,
    part,
    far_out,
    far_in,
    sum_out,
    sum_in,
    in_sem,
    own_sem,
    doc_sem,
    own_send,
    near_recv,
    fwd_send,
    far_recv,
    back_send,
    back_recv,
    sum_send,
    sum_recv,
):
    place = lax.axis_index("outer") * inner_count + lax.axis_index("inner")
    total = outer_count * inner_count
    has_prev = place >= 1
    has_prev2 = place >= 2
    has_next = place <= total - 2
    has_both = has_prev & has_next
    after = jnp.minimum(place + 1, total - 1)
    before = jnp.maximum(place - 1, 0)
    next_id = (after // inner_count, lax.rem(after, inner_count))
    prev_id = (before // inner_count, lax.rem(before, inner_count))

    def remote(src, dst, send, recv, device):
        return pltpu.make_async_remote_copy(
            src_ref=src,
            dst_ref=dst,
            send_sem=send,
            recv_sem=recv,
            device_id=device,
            device_id_type=MESH,
        )

    def own_copy(h, which):
        source = (k_hbm, v_hbm)[which]
        return remote(
            source.at[:, columns(h, HEAD_SIZE)],
            kv.at[h, which, 1],
            own_send.at[h, which],
            near_recv.at[h, which],
            next_id,
        )

    def forward_copy(h, which):
        return remote(
            kv.at[h, which, 1],
            kv.at[h, which, 2],
            fwd_send.at[h, which],
            far_recv.at[h, which],
            next_id,
        )

    def back_copy(h, which):
        return remote(
            far_out.at[h, which],
            far_in.at[h, which],
            back_send.at[h, which],
            back_recv.at[h, which],
            prev_id,
        )

    def sum_copy(h, which):
        return remote(
            sum_out.at[h, which],
            sum_in.at[h, which],
            sum_send.at[h, which],
            sum_recv.at[h, which],
            prev_id,
        )

    def load_copies(h):
        wide = columns(h, WIDE)
        narrow = columns(h, HEAD_SIZE)
        return (
            pltpu.make_async_copy(q_hbm.at[:, wide], q.at[:, wide], in_sem.at[h, 0]),
            pltpu.make_async_copy(g_hbm.at[:, wide], g.at[:, wide], in_sem.at[h, 1]),
            pltpu.make_async_copy(k_hbm.at[:, narrow], kv.at[h, 0, 0], own_sem.at[h, 0]),
            pltpu.make_async_copy(v_hbm.at[:, narrow], kv.at[h, 1, 0], own_sem.at[h, 1]),
        )

    doc_copy = pltpu.make_async_copy(doc_hbm, docs, doc_sem)
    doc_copy.start()

    barrier = pltpu.get_barrier_semaphore()

    @pl.when(has_prev)
    def _():
        pl.semaphore_signal(barrier, inc=1, device_id=prev_id, device_id_type=MESH)

    @pl.when(has_next)
    def _():
        pl.semaphore_wait(barrier, 1)

    lead_in = INIT + jnp.where(lax.axis_index("inner") < EARLY, EXTRA, 0)

    def send_own(h):
        @pl.when(has_next)
        def _():
            for which in BOTH:
                own_copy(h, which).start()

    def pass_on(h):
        @pl.when(has_prev)
        def _():
            for which in BOTH:
                own_copy(h, which).wait_recv()

                @pl.when(has_next)
                def _():
                    forward_copy(h, which).start()

    def start_own(h, carry):
        send_own(h)
        return carry

    lax.fori_loop(0, lead_in, start_own, 0)

    def start_loads(h, carry):
        for copy in load_copies(h):
            copy.start()
        return carry

    lax.fori_loop(0, LOADS, start_loads, 0)

    @pl.when(place <= 1)
    def _():
        blank = jnp.zeros((HEADS, 2, BLOCK, HEAD_SIZE), jnp.bfloat16)
        kv[:, :, 2] = blank

        @pl.when(place == 0)
        def _():
            kv[:, :, 1] = blank

    @pl.when(place == total - 1)
    def _():
        far_in[...] = jnp.zeros_like(far_in)
        sum_in[...] = jnp.zeros_like(sum_in)

    doc_copy.wait()
    own_labels = jnp.broadcast_to(docs[pl.ds(place, 1), :], (BLOCK, BLOCK)).T
    for which in range(3):
        row = docs[pl.ds(jnp.maximum(place - which, 0), 1), :]
        allowed = jnp.broadcast_to(row, (BLOCK, BLOCK)) == own_labels
        if which == 0:
            query_place = lax.broadcasted_iota(jnp.int32, (BLOCK, BLOCK), 0)
            key_place = lax.broadcasted_iota(jnp.int32, (BLOCK, BLOCK), 1)
            allowed = allowed & (key_place <= query_place)
        else:
            allowed = allowed & jnp.broadcast_to(place >= which, (BLOCK, BLOCK))
        bias[:, which * BLOCK : (which + 1) * BLOCK] = jnp.where(allowed, 0.0, NEG)

    def combine(h):
        @pl.when(has_prev)
        def _():
            for which in (1, 0):

                @pl.when(has_next)
                def _():
                    back_copy(h, which).wait_recv()

                sum_out[h, which] = (
                    part[h, which, 1] + far_in[h, which].astype(jnp.float32)
                ).astype(jnp.bfloat16)
                sum_copy(h, which).start()

    def finish(h):
        for which in (1, 0):

            @pl.when(has_next)
            def _():
                sum_copy(h, which).wait_recv()

            (dk, dv)[which][:, columns(h, HEAD_SIZE)] = (
                part[h, which, 0] + sum_in[h, which].astype(jnp.float32)
            ).astype(jnp.bfloat16)

    def next_own(h):
        @pl.when(h + LEAD + lead_in < HEADS)
        def _():
            send_own(h + LEAD + lead_in)

    def go_on(h):
        @pl.when(h + LEAD < HEADS)
        def _():
            pass_on(h + LEAD)

        next_own(h)

    def wait_far(h):
        @pl.when(has_prev2)
        def _():
            for which in BOTH:
                forward_copy(h, which).wait_recv()

    def combine_late(h):
        @pl.when(h >= LAG)
        def _():
            combine(h - LAG)

    def attend(h):

        def rows(ref):
            return jnp.concatenate(
                [ref[:, columns(h * GROUP + n, HEAD_SIZE)] for n in range(GROUP)], axis=0
            )

        query, grad = rows(q), rows(g)
        keys = kv[h, 0].reshape(3 * BLOCK, HEAD_SIZE)
        values = kv[h, 1].reshape(3 * BLOCK, HEAD_SIZE)
        scores = dot_of(query, keys, NT)
        grad_weights = dot_of(grad, values, NT)
        scores = scores * (SCALING * LOG2E) + jnp.concatenate([bias[...]] * GROUP, axis=0)
        top = jnp.max(scores, axis=1, keepdims=True)
        weights = jnp.exp2(scores - top)
        sums = jnp.sum(weights, axis=1, keepdims=True)
        probs = weights * (1.0 / sums)
        coarse = probs.astype(jnp.bfloat16)
        products = probs * grad_weights
        row_dot = jnp.sum(products, axis=1, keepdims=True)
        grad_scores = (products - probs * row_dot).astype(jnp.bfloat16)
        far_out[h, 1] = dot_of(coarse[:, 2 * BLOCK :], grad, TN).astype(jnp.bfloat16)
        far_out[h, 0] = (dot_of(grad_scores[:, 2 * BLOCK :], query, TN) * SCALING).astype(
            jnp.bfloat16
        )

        @pl.when(has_prev2)
        def _():
            for which in (1, 0):
                back_copy(h, which).start()

        go_on(h)
        value_part = dot_of(coarse[:, : 2 * BLOCK], grad, TN)
        key_part = dot_of(grad_scores[:, : 2 * BLOCK], query, TN) * SCALING
        for which, value in ((0, key_part), (1, value_part)):
            part[h, which] = value.reshape(2, BLOCK, HEAD_SIZE)
        attended = dot(coarse, values).astype(jnp.bfloat16)
        query_grad = (dot(grad_scores, keys) * SCALING).astype(jnp.bfloat16)
        for n in range(GROUP):
            place_of = columns(h * GROUP + n, HEAD_SIZE)
            att[:, place_of] = attended[n * BLOCK : (n + 1) * BLOCK]
            dq[:, place_of] = query_grad[n * BLOCK : (n + 1) * BLOCK]

    for h in range(LEAD):
        pass_on(h)
        send_own(h + lead_in)

    def step(h, carry):
        for copy in load_copies(h):
            copy.wait()

        @pl.when(h + LOADS < HEADS)
        def _():
            start_loads(h + LOADS, 0)

        wait_far(h)
        attend(h)

        combine_late(h)

        @pl.when(h >= FINAL)
        def _():
            finish(h - FINAL)

        return carry

    lax.fori_loop(0, HEADS, step, 0)
    for late in range(LAG, 0, -1):
        combine(HEADS - late)
    for late in range(FINAL, 0, -1):
        finish(HEADS - late)

    def drain(h, carry):
        for which in BOTH:

            @pl.when(has_next)
            def _():
                own_copy(h, which).wait_send()

            @pl.when(has_both)
            def _():
                forward_copy(h, which).wait_send()

            @pl.when(has_prev2)
            def _():
                back_copy(h, which).wait_send()

            @pl.when(has_prev)
            def _():
                sum_copy(h, which).wait_send()

        return carry

    lax.fori_loop(0, HEADS, drain, 0)


def store_kernel(*refs):
    sources, targets, sems = refs[:4], refs[4:8], refs[8]
    rows = BLOCK // SPLIT
    copies = [
        pltpu.make_async_copy(
            source.at[pl.ds(m * rows, rows)], target.at[pl.ds(m * rows, rows)], sems.at[n, m]
        )
        for n, (source, target) in enumerate(zip(sources, targets))
        for m in range(SPLIT)
    ]
    for copy in copies:
        copy.start()
    for copy in copies:
        copy.wait()


def body(outer_count, inner_count, query_matrix, key_matrix, value_matrix, output_gradient, doc_ids):
    hbm = pl.BlockSpec(memory_space=pltpu.HBM)
    vmem = pl.BlockSpec(memory_space=pltpu.VMEM)
    labels = doc_ids.reshape(doc_ids.shape[0] // BLOCK, BLOCK)
    tile = (BLOCK, HEAD_SIZE)
    bf16, f32 = jnp.bfloat16, jnp.float32
    dma = pltpu.SemaphoreType.DMA
    shapes = [query_matrix.shape, query_matrix.shape, key_matrix.shape, value_matrix.shape]
    operands = [
        pltpu.with_memory_space_constraint(operand, pltpu.HBM)
        for operand in (query_matrix, key_matrix, value_matrix, output_gradient, labels)
    ]
    results = pl.pallas_call(
        functools.partial(kernel, outer_count, inner_count),
        out_shape=[pltpu.VMEM(shape, bf16) for shape in shapes],
        in_specs=[hbm] * 5,
        out_specs=[vmem] * 4,
        scratch_shapes=[
            pltpu.VMEM(query_matrix.shape, bf16),
            pltpu.VMEM(query_matrix.shape, bf16),
            pltpu.VMEM(labels.shape, jnp.int32),
            pltpu.VMEM((BLOCK, 3 * BLOCK), f32),
            pltpu.VMEM((HEADS, 2, 3) + tile, bf16),
            pltpu.VMEM((HEADS, 2, 2) + tile, f32),
        ]
        + [pltpu.VMEM((HEADS, 2) + tile, bf16)] * 4
        + [dma((HEADS, 2)), dma((HEADS, 2)), dma(())]
        + [dma((HEADS, 2))] * 8,
        compiler_params=pltpu.CompilerParams(
            collective_id=0, has_side_effects=True, vmem_limit_bytes=44 * 1024 * 1024
        ),
    )(*operands)
    results = [pltpu.with_memory_space_constraint(result, pltpu.VMEM) for result in results]
    return pl.pallas_call(
        store_kernel,
        out_shape=[jax.ShapeDtypeStruct(shape, bf16) for shape in shapes],
        in_specs=[vmem] * 4,
        out_specs=[pl.BlockSpec(memory_space=pltpu.HBM)] * 4,
        scratch_shapes=[dma((4, SPLIT))],
        compiler_params=pltpu.CompilerParams(vmem_limit_bytes=1024 * 1024),
    )(*results)


def solution(mesh):
    split = P(("outer", "inner"), None)
    return jax.shard_map(
        functools.partial(body, mesh.shape["outer"], mesh.shape["inner"]),
        mesh=mesh,
        in_specs=(split, split, split, split, P()),
        out_specs=(split, split, split, split),
        check_vma=False,
    )
```

```python
import functools

import jax
import jax.numpy as jnp
from jax import lax
from jax.experimental import pallas as pl
from jax.experimental.pallas import tpu as pltpu
from jax.sharding import PartitionSpec as P

HEADS = 8
GROUP = 8
HEAD_SIZE = 128
BLOCK = 128
WIDE = GROUP * HEAD_SIZE
NEG = -1e30
SCALING = HEAD_SIZE**-0.5
LOG2E = 1.4426950408889634
MESH = pl.DeviceIdType.MESH
BOTH = (0, 1)
INIT = 2
LEAD = 2
LAG = 2
FINAL = 4
LOADS = 2
EXTRA = 2
EARLY = 1
SPLIT = 2

NT = (((1,), (1,)), ((), ()))
TN = (((0,), (0,)), ((), ()))


def dot(a, b):
    return jnp.dot(a, b, preferred_element_type=jnp.float32)


def dot_of(a, b, dims):
    return lax.dot_general(a, b, dims, preferred_element_type=jnp.float32)


def columns(head, width):
    return pl.ds(pl.multiple_of(head * width, width), width)


def kernel(
    outer_count,
    inner_count,
    q_hbm,
    k_hbm,
    v_hbm,
    g_hbm,
    doc_hbm,
    att,
    dq,
    dk,
    dv,
    q,
    g,
    docs,
    bias,
    kv,
    part,
    far_out,
    far_in,
    sum_out,
    sum_in,
    in_sem,
    own_sem,
    doc_sem,
    own_send,
    near_recv,
    fwd_send,
    far_recv,
    back_send,
    back_recv,
    sum_send,
    sum_recv,
):
    place = lax.axis_index("outer") * inner_count + lax.axis_index("inner")
    total = outer_count * inner_count
    has_prev = place >= 1
    has_prev2 = place >= 2
    has_next = place <= total - 2
    has_both = has_prev & has_next
    after = jnp.minimum(place + 1, total - 1)
    before = jnp.maximum(place - 1, 0)
    next_id = (after // inner_count, lax.rem(after, inner_count))
    prev_id = (before // inner_count, lax.rem(before, inner_count))

    def remote(src, dst, send, recv, device):
        return pltpu.make_async_remote_copy(
            src_ref=src,
            dst_ref=dst,
            send_sem=send,
            recv_sem=recv,
            device_id=device,
            device_id_type=MESH,
        )

    def own_copy(h, which):
        source = (k_hbm, v_hbm)[which]
        return remote(
            source.at[:, columns(h, HEAD_SIZE)],
            kv.at[h, which, 1],
            own_send.at[h, which],
            near_recv.at[h, which],
            next_id,
        )

    def forward_copy(h, which):
        return remote(
            kv.at[h, which, 1],
            kv.at[h, which, 2],
            fwd_send.at[h, which],
            far_recv.at[h, which],
            next_id,
        )

    def back_copy(h, which):
        return remote(
            far_out.at[h, which],
            far_in.at[h, which],
            back_send.at[h, which],
            back_recv.at[h, which],
            prev_id,
        )

    def sum_copy(h, which):
        return remote(
            sum_out.at[h, which],
            sum_in.at[h, which],
            sum_send.at[h, which],
            sum_recv.at[h, which],
            prev_id,
        )

    def load_copies(h):
        wide = columns(h, WIDE)
        narrow = columns(h, HEAD_SIZE)
        return (
            pltpu.make_async_copy(q_hbm.at[:, wide], q.at[:, wide], in_sem.at[h, 0]),
            pltpu.make_async_copy(g_hbm.at[:, wide], g.at[:, wide], in_sem.at[h, 1]),
            pltpu.make_async_copy(k_hbm.at[:, narrow], kv.at[h, 0, 0], own_sem.at[h, 0]),
            pltpu.make_async_copy(v_hbm.at[:, narrow], kv.at[h, 1, 0], own_sem.at[h, 1]),
        )

    doc_copy = pltpu.make_async_copy(doc_hbm, docs, doc_sem)
    doc_copy.start()

    barrier = pltpu.get_barrier_semaphore()

    @pl.when(has_prev)
    def _():
        pl.semaphore_signal(barrier, inc=1, device_id=prev_id, device_id_type=MESH)

    @pl.when(has_next)
    def _():
        pl.semaphore_wait(barrier, 1)

    lead_in = INIT + jnp.where(lax.axis_index("inner") < EARLY, EXTRA, 0)

    def send_own(h):
        @pl.when(has_next)
        def _():
            for which in BOTH:
                own_copy(h, which).start()

    def pass_on(h):
        @pl.when(has_prev)
        def _():
            for which in BOTH:
                own_copy(h, which).wait_recv()

                @pl.when(has_next)
                def _():
                    forward_copy(h, which).start()

    def start_own(h, carry):
        send_own(h)
        return carry

    lax.fori_loop(0, lead_in, start_own, 0)

    def start_loads(h, carry):
        for copy in load_copies(h):
            copy.start()
        return carry

    lax.fori_loop(0, LOADS, start_loads, 0)

    @pl.when(place <= 1)
    def _():
        blank = jnp.zeros((HEADS, 2, BLOCK, HEAD_SIZE), jnp.bfloat16)
        kv[:, :, 2] = blank

        @pl.when(place == 0)
        def _():
            kv[:, :, 1] = blank

    @pl.when(place == total - 1)
    def _():
        far_in[...] = jnp.zeros_like(far_in)
        sum_in[...] = jnp.zeros_like(sum_in)

    doc_copy.wait()
    own_labels = jnp.broadcast_to(docs[pl.ds(place, 1), :], (BLOCK, BLOCK)).T
    for which in range(3):
        row = docs[pl.ds(jnp.maximum(place - which, 0), 1), :]
        allowed = jnp.broadcast_to(row, (BLOCK, BLOCK)) == own_labels
        if which == 0:
            query_place = lax.broadcasted_iota(jnp.int32, (BLOCK, BLOCK), 0)
            key_place = lax.broadcasted_iota(jnp.int32, (BLOCK, BLOCK), 1)
            allowed = allowed & (key_place <= query_place)
        else:
            allowed = allowed & jnp.broadcast_to(place >= which, (BLOCK, BLOCK))
        bias[:, which * BLOCK : (which + 1) * BLOCK] = jnp.where(allowed, 0.0, NEG)

    def combine(h):
        @pl.when(has_prev)
        def _():
            for which in (1, 0):

                @pl.when(has_next)
                def _():
                    back_copy(h, which).wait_recv()

                sum_out[h, which] = (
                    part[h, which, 1] + far_in[h, which].astype(jnp.float32)
                ).astype(jnp.bfloat16)
                sum_copy(h, which).start()

    def finish(h):
        for which in (1, 0):

            @pl.when(has_next)
            def _():
                sum_copy(h, which).wait_recv()

            (dk, dv)[which][:, columns(h, HEAD_SIZE)] = (
                part[h, which, 0] + sum_in[h, which].astype(jnp.float32)
            ).astype(jnp.bfloat16)

    def next_own(h):
        @pl.when(h + LEAD + lead_in < HEADS)
        def _():
            send_own(h + LEAD + lead_in)

    def go_on(h):
        @pl.when(h + LEAD < HEADS)
        def _():
            pass_on(h + LEAD)

        next_own(h)

    def wait_far(h):
        @pl.when(has_prev2)
        def _():
            for which in BOTH:
                forward_copy(h, which).wait_recv()

    def combine_late(h):
        @pl.when(h >= LAG)
        def _():
            combine(h - LAG)

    def attend(h):

        def rows(ref):
            return jnp.concatenate(
                [ref[:, columns(h * GROUP + n, HEAD_SIZE)] for n in range(GROUP)], axis=0
            )

        query, grad = rows(q), rows(g)
        keys = kv[h, 0].reshape(3 * BLOCK, HEAD_SIZE)
        values = kv[h, 1].reshape(3 * BLOCK, HEAD_SIZE)
        scores = dot_of(query, keys, NT)
        grad_weights = dot_of(grad, values, NT)
        scores = scores * (SCALING * LOG2E) + jnp.concatenate([bias[...]] * GROUP, axis=0)
        top = jnp.max(scores, axis=1, keepdims=True)
        weights = jnp.exp2(scores - top)
        sums = jnp.sum(weights, axis=1, keepdims=True)
        probs = weights * (1.0 / sums)
        coarse = probs.astype(jnp.bfloat16)
        products = probs * grad_weights
        row_dot = jnp.sum(products, axis=1, keepdims=True)
        grad_scores = (products - probs * row_dot).astype(jnp.bfloat16)
        far_out[h, 1] = dot_of(coarse[:, 2 * BLOCK :], grad, TN).astype(jnp.bfloat16)
        far_out[h, 0] = (dot_of(grad_scores[:, 2 * BLOCK :], query, TN) * SCALING).astype(
            jnp.bfloat16
        )

        @pl.when(has_prev2)
        def _():
            for which in (1, 0):
                back_copy(h, which).start()

        go_on(h)
        value_part = dot_of(coarse[:, : 2 * BLOCK], grad, TN)
        key_part = dot_of(grad_scores[:, : 2 * BLOCK], query, TN) * SCALING
        for which, value in ((0, key_part), (1, value_part)):
            part[h, which] = value.reshape(2, BLOCK, HEAD_SIZE)
        attended = dot(coarse, values).astype(jnp.bfloat16)
        query_grad = (dot(grad_scores, keys) * SCALING).astype(jnp.bfloat16)
        for n in range(GROUP):
            place_of = columns(h * GROUP + n, HEAD_SIZE)
            att[:, place_of] = attended[n * BLOCK : (n + 1) * BLOCK]
            dq[:, place_of] = query_grad[n * BLOCK : (n + 1) * BLOCK]

    for h in range(LEAD):
        pass_on(h)
        send_own(h + lead_in)

    def step(h, carry):
        for copy in load_copies(h):
            copy.wait()

        @pl.when(h + LOADS < HEADS)
        def _():
            start_loads(h + LOADS, 0)

        wait_far(h)
        attend(h)

        combine_late(h)

        @pl.when(h >= FINAL)
        def _():
            finish(h - FINAL)

        return carry

    lax.fori_loop(0, HEADS, step, 0)

    def drain_forward(h, carry):
        for which in BOTH:

            @pl.when(has_next)
            def _():
                own_copy(h, which).wait_send()

            @pl.when(has_both)
            def _():
                forward_copy(h, which).wait_send()

        return carry

    def drain_back(h, carry):
        for which in BOTH:

            @pl.when(has_prev2)
            def _():
                back_copy(h, which).wait_send()

            @pl.when(has_prev)
            def _():
                sum_copy(h, which).wait_send()

        return carry

    for late in range(LAG, 1, -1):
        combine(HEADS - late)
    lax.fori_loop(0, HEADS, drain_forward, 0)
    lax.fori_loop(0, HEADS - FINAL, drain_back, 0)
    finish(HEADS - FINAL)
    combine(HEADS - 1)
    for late in range(FINAL - 1, 0, -1):
        finish(HEADS - late)
    lax.fori_loop(HEADS - FINAL, HEADS, drain_back, 0)


def store_kernel(*refs):
    sources, targets, sems = refs[:4], refs[4:8], refs[8]
    rows = BLOCK // SPLIT
    copies = [
        pltpu.make_async_copy(
            source.at[pl.ds(m * rows, rows)], target.at[pl.ds(m * rows, rows)], sems.at[n, m]
        )
        for n, (source, target) in enumerate(zip(sources, targets))
        for m in range(SPLIT)
    ]
    for copy in copies:
        copy.start()
    for copy in copies:
        copy.wait()


def body(outer_count, inner_count, query_matrix, key_matrix, value_matrix, output_gradient, doc_ids):
    hbm = pl.BlockSpec(memory_space=pltpu.HBM)
    vmem = pl.BlockSpec(memory_space=pltpu.VMEM)
    labels = doc_ids.reshape(doc_ids.shape[0] // BLOCK, BLOCK)
    tile = (BLOCK, HEAD_SIZE)
    bf16, f32 = jnp.bfloat16, jnp.float32
    dma = pltpu.SemaphoreType.DMA
    shapes = [query_matrix.shape, query_matrix.shape, key_matrix.shape, value_matrix.shape]
    operands = [
        pltpu.with_memory_space_constraint(operand, pltpu.HBM)
        for operand in (query_matrix, key_matrix, value_matrix, output_gradient, labels)
    ]
    results = pl.pallas_call(
        functools.partial(kernel, outer_count, inner_count),
        out_shape=[pltpu.VMEM(shape, bf16) for shape in shapes],
        in_specs=[hbm] * 5,
        out_specs=[vmem] * 4,
        scratch_shapes=[
            pltpu.VMEM(query_matrix.shape, bf16),
            pltpu.VMEM(query_matrix.shape, bf16),
            pltpu.VMEM(labels.shape, jnp.int32),
            pltpu.VMEM((BLOCK, 3 * BLOCK), f32),
            pltpu.VMEM((HEADS, 2, 3) + tile, bf16),
            pltpu.VMEM((HEADS, 2, 2) + tile, f32),
        ]
        + [pltpu.VMEM((HEADS, 2) + tile, bf16)] * 4
        + [dma((HEADS, 2)), dma((HEADS, 2)), dma(())]
        + [dma((HEADS, 2))] * 8,
        compiler_params=pltpu.CompilerParams(
            collective_id=0, has_side_effects=True, vmem_limit_bytes=44 * 1024 * 1024
        ),
    )(*operands)
    results = [pltpu.with_memory_space_constraint(result, pltpu.VMEM) for result in results]
    return pl.pallas_call(
        store_kernel,
        out_shape=[jax.ShapeDtypeStruct(shape, bf16) for shape in shapes],
        in_specs=[vmem] * 4,
        out_specs=[pl.BlockSpec(memory_space=pltpu.HBM)] * 4,
        scratch_shapes=[dma((4, SPLIT))],
        compiler_params=pltpu.CompilerParams(vmem_limit_bytes=1024 * 1024),
    )(*results)


def solution(mesh):
    split = P(("outer", "inner"), None)
    return jax.shard_map(
        functools.partial(body, mesh.shape["outer"], mesh.shape["inner"]),
        mesh=mesh,
        in_specs=(split, split, split, split, P()),
        out_specs=(split, split, split, split),
        check_vma=False,
    )
```

```python
import functools

import jax
import jax.numpy as jnp
from jax import lax
from jax.experimental import pallas as pl
from jax.experimental.pallas import tpu as pltpu
from jax.sharding import PartitionSpec as P

HEADS = 8
GROUP = 8
HEAD_SIZE = 128
BLOCK = 128
WIDE = GROUP * HEAD_SIZE
NEG = -1e30
SCALING = HEAD_SIZE**-0.5
LOG2E = 1.4426950408889634
MESH = pl.DeviceIdType.MESH
BOTH = (0, 1)
INIT = 2
LEAD = 2
LAG = 2
FINAL = 4
LOADS = 2
EXTRA = 2
EARLY = 1
SPLIT = 2

NT = (((1,), (1,)), ((), ()))
TN = (((0,), (0,)), ((), ()))


def dot(a, b):
    return jnp.dot(a, b, preferred_element_type=jnp.float32)


def dot_of(a, b, dims):
    return lax.dot_general(a, b, dims, preferred_element_type=jnp.float32)


def columns(head, width):
    return pl.ds(pl.multiple_of(head * width, width), width)


def kernel(
    outer_count,
    inner_count,
    q_hbm,
    k_hbm,
    v_hbm,
    g_hbm,
    doc_hbm,
    att,
    dq,
    dk,
    dv,
    q,
    g,
    docs,
    bias,
    kv,
    part,
    far_out,
    far_in,
    sum_out,
    sum_in,
    in_sem,
    own_sem,
    doc_sem,
    own_send,
    near_recv,
    fwd_send,
    far_recv,
    back_send,
    back_recv,
    sum_send,
    sum_recv,
):
    place = lax.axis_index("outer") * inner_count + lax.axis_index("inner")
    total = outer_count * inner_count
    has_prev = place >= 1
    has_prev2 = place >= 2
    has_next = place <= total - 2
    has_both = has_prev & has_next
    after = jnp.minimum(place + 1, total - 1)
    before = jnp.maximum(place - 1, 0)
    next_id = (after // inner_count, lax.rem(after, inner_count))
    prev_id = (before // inner_count, lax.rem(before, inner_count))

    def remote(src, dst, send, recv, device):
        return pltpu.make_async_remote_copy(
            src_ref=src,
            dst_ref=dst,
            send_sem=send,
            recv_sem=recv,
            device_id=device,
            device_id_type=MESH,
        )

    def own_copy(h, which):
        source = (k_hbm, v_hbm)[which]
        return remote(
            source.at[:, columns(h, HEAD_SIZE)],
            kv.at[h, which, 1],
            own_send.at[h, which],
            near_recv.at[h, which],
            next_id,
        )

    def forward_copy(h, which):
        return remote(
            kv.at[h, which, 1],
            kv.at[h, which, 2],
            fwd_send.at[h, which],
            far_recv.at[h, which],
            next_id,
        )

    def back_copy(h, which):
        return remote(
            far_out.at[h, which],
            far_in.at[h, which],
            back_send.at[h, which],
            back_recv.at[h, which],
            prev_id,
        )

    def sum_copy(h, which):
        return remote(
            sum_out.at[h, which],
            sum_in.at[h, which],
            sum_send.at[h, which],
            sum_recv.at[h, which],
            prev_id,
        )

    def load_copies(h):
        wide = columns(h, WIDE)
        narrow = columns(h, HEAD_SIZE)
        return (
            pltpu.make_async_copy(q_hbm.at[:, wide], q.at[:, wide], in_sem.at[h, 0]),
            pltpu.make_async_copy(g_hbm.at[:, wide], g.at[:, wide], in_sem.at[h, 1]),
            pltpu.make_async_copy(k_hbm.at[:, narrow], kv.at[h, 0, 0], own_sem.at[h, 0]),
            pltpu.make_async_copy(v_hbm.at[:, narrow], kv.at[h, 1, 0], own_sem.at[h, 1]),
        )

    doc_copy = pltpu.make_async_copy(doc_hbm, docs, doc_sem)
    doc_copy.start()

    barrier = pltpu.get_barrier_semaphore()

    @pl.when(has_prev)
    def _():
        pl.semaphore_signal(barrier, inc=1, device_id=prev_id, device_id_type=MESH)

    @pl.when(has_next)
    def _():
        pl.semaphore_wait(barrier, 1)

    lead_in = INIT + jnp.where(lax.axis_index("inner") < EARLY, EXTRA, 0)

    def send_own(h):
        @pl.when(has_next)
        def _():
            for which in BOTH:
                own_copy(h, which).start()

    def pass_on(h):
        @pl.when(has_prev)
        def _():
            for which in BOTH:
                own_copy(h, which).wait_recv()

                @pl.when(has_next)
                def _():
                    forward_copy(h, which).start()

    def start_own(h, carry):
        send_own(h)
        return carry

    lax.fori_loop(0, lead_in, start_own, 0)

    def start_loads(h, carry):
        for copy in load_copies(h):
            copy.start()
        return carry

    lax.fori_loop(0, LOADS, start_loads, 0)

    @pl.when(place <= 1)
    def _():
        blank = jnp.zeros((HEADS, 2, BLOCK, HEAD_SIZE), jnp.bfloat16)
        kv[:, :, 2] = blank

        @pl.when(place == 0)
        def _():
            kv[:, :, 1] = blank

    @pl.when(place == total - 1)
    def _():
        far_in[...] = jnp.zeros_like(far_in)
        sum_in[...] = jnp.zeros_like(sum_in)

    doc_copy.wait()
    own_labels = jnp.broadcast_to(docs[pl.ds(place, 1), :], (BLOCK, BLOCK)).T
    for which in range(3):
        row = docs[pl.ds(jnp.maximum(place - which, 0), 1), :]
        allowed = jnp.broadcast_to(row, (BLOCK, BLOCK)) == own_labels
        if which == 0:
            query_place = lax.broadcasted_iota(jnp.int32, (BLOCK, BLOCK), 0)
            key_place = lax.broadcasted_iota(jnp.int32, (BLOCK, BLOCK), 1)
            allowed = allowed & (key_place <= query_place)
        else:
            allowed = allowed & jnp.broadcast_to(place >= which, (BLOCK, BLOCK))
        bias[:, which * BLOCK : (which + 1) * BLOCK] = jnp.where(allowed, 0.0, NEG)

    def combine(h):
        @pl.when(has_prev)
        def _():
            for which in (1, 0):

                @pl.when(has_next)
                def _():
                    back_copy(h, which).wait_recv()

                sum_out[h, which] = (
                    part[h, which, 1] + far_in[h, which].astype(jnp.float32)
                ).astype(jnp.bfloat16)
                sum_copy(h, which).start()

    def finish(h):
        for which in (1, 0):

            @pl.when(has_next)
            def _():
                sum_copy(h, which).wait_recv()

            (dk, dv)[which][:, columns(h, HEAD_SIZE)] = (
                part[h, which, 0] + sum_in[h, which].astype(jnp.float32)
            ).astype(jnp.bfloat16)

    def next_own(h):
        @pl.when(h + LEAD + lead_in < HEADS)
        def _():
            send_own(h + LEAD + lead_in)

    def go_on(h):
        @pl.when(h + LEAD < HEADS)
        def _():
            pass_on(h + LEAD)

        next_own(h)

    def wait_far(h, which):
        @pl.when(has_prev2)
        def _():
            forward_copy(h, which).wait_recv()

    def combine_late(h):
        @pl.when(h >= LAG)
        def _():
            combine(h - LAG)

    def attend(h):

        def rows(ref):
            return jnp.concatenate(
                [ref[:, columns(h * GROUP + n, HEAD_SIZE)] for n in range(GROUP)], axis=0
            )

        query, grad = rows(q), rows(g)
        wait_far(h, 0)
        keys = kv[h, 0].reshape(3 * BLOCK, HEAD_SIZE)
        scores = dot_of(query, keys, NT)
        scores = scores * (SCALING * LOG2E) + jnp.concatenate([bias[...]] * GROUP, axis=0)
        wait_far(h, 1)
        values = kv[h, 1].reshape(3 * BLOCK, HEAD_SIZE)
        grad_weights = dot_of(grad, values, NT)
        top = jnp.max(scores, axis=1, keepdims=True)
        weights = jnp.exp2(scores - top)
        sums = jnp.sum(weights, axis=1, keepdims=True)
        probs = weights * (1.0 / sums)
        coarse = probs.astype(jnp.bfloat16)
        products = probs * grad_weights
        row_dot = jnp.sum(products, axis=1, keepdims=True)
        grad_scores = (products - probs * row_dot).astype(jnp.bfloat16)
        far_out[h, 1] = dot_of(coarse[:, 2 * BLOCK :], grad, TN).astype(jnp.bfloat16)
        far_out[h, 0] = (dot_of(grad_scores[:, 2 * BLOCK :], query, TN) * SCALING).astype(
            jnp.bfloat16
        )

        @pl.when(has_prev2)
        def _():
            for which in (1, 0):
                back_copy(h, which).start()

        go_on(h)
        value_part = dot_of(coarse[:, : 2 * BLOCK], grad, TN)
        key_part = dot_of(grad_scores[:, : 2 * BLOCK], query, TN) * SCALING
        for which, value in ((0, key_part), (1, value_part)):
            part[h, which] = value.reshape(2, BLOCK, HEAD_SIZE)
        attended = dot(coarse, values).astype(jnp.bfloat16)
        query_grad = (dot(grad_scores, keys) * SCALING).astype(jnp.bfloat16)
        for n in range(GROUP):
            place_of = columns(h * GROUP + n, HEAD_SIZE)
            att[:, place_of] = attended[n * BLOCK : (n + 1) * BLOCK]
            dq[:, place_of] = query_grad[n * BLOCK : (n + 1) * BLOCK]

    for h in range(LEAD):
        pass_on(h)
        send_own(h + lead_in)

    def step(h, carry):
        for copy in load_copies(h):
            copy.wait()

        @pl.when(h + LOADS < HEADS)
        def _():
            start_loads(h + LOADS, 0)

        attend(h)

        combine_late(h)

        @pl.when(h >= FINAL)
        def _():
            finish(h - FINAL)

        return carry

    lax.fori_loop(0, HEADS, step, 0)

    def drain_forward(h, carry):
        for which in BOTH:

            @pl.when(has_next)
            def _():
                own_copy(h, which).wait_send()

            @pl.when(has_both)
            def _():
                forward_copy(h, which).wait_send()

        return carry

    def drain_back(h, carry):
        for which in BOTH:

            @pl.when(has_prev2)
            def _():
                back_copy(h, which).wait_send()

            @pl.when(has_prev)
            def _():
                sum_copy(h, which).wait_send()

        return carry

    for late in range(LAG, 1, -1):
        combine(HEADS - late)
    lax.fori_loop(0, HEADS, drain_forward, 0)
    lax.fori_loop(0, HEADS - FINAL, drain_back, 0)
    finish(HEADS - FINAL)
    combine(HEADS - 1)
    for late in range(FINAL - 1, 0, -1):
        finish(HEADS - late)
    lax.fori_loop(HEADS - FINAL, HEADS, drain_back, 0)


def store_kernel(*refs):
    sources, targets, sems = refs[:4], refs[4:8], refs[8]
    rows = BLOCK // SPLIT
    copies = [
        pltpu.make_async_copy(
            source.at[pl.ds(m * rows, rows)], target.at[pl.ds(m * rows, rows)], sems.at[n, m]
        )
        for n, (source, target) in enumerate(zip(sources, targets))
        for m in range(SPLIT)
    ]
    for copy in copies:
        copy.start()
    for copy in copies:
        copy.wait()


def body(outer_count, inner_count, query_matrix, key_matrix, value_matrix, output_gradient, doc_ids):
    hbm = pl.BlockSpec(memory_space=pltpu.HBM)
    vmem = pl.BlockSpec(memory_space=pltpu.VMEM)
    labels = doc_ids.reshape(doc_ids.shape[0] // BLOCK, BLOCK)
    tile = (BLOCK, HEAD_SIZE)
    bf16, f32 = jnp.bfloat16, jnp.float32
    dma = pltpu.SemaphoreType.DMA
    shapes = [query_matrix.shape, query_matrix.shape, key_matrix.shape, value_matrix.shape]
    operands = [
        pltpu.with_memory_space_constraint(operand, pltpu.HBM)
        for operand in (query_matrix, key_matrix, value_matrix, output_gradient, labels)
    ]
    results = pl.pallas_call(
        functools.partial(kernel, outer_count, inner_count),
        out_shape=[pltpu.VMEM(shape, bf16) for shape in shapes],
        in_specs=[hbm] * 5,
        out_specs=[vmem] * 4,
        scratch_shapes=[
            pltpu.VMEM(query_matrix.shape, bf16),
            pltpu.VMEM(query_matrix.shape, bf16),
            pltpu.VMEM(labels.shape, jnp.int32),
            pltpu.VMEM((BLOCK, 3 * BLOCK), f32),
            pltpu.VMEM((HEADS, 2, 3) + tile, bf16),
            pltpu.VMEM((HEADS, 2, 2) + tile, f32),
        ]
        + [pltpu.VMEM((HEADS, 2) + tile, bf16)] * 4
        + [dma((HEADS, 2)), dma((HEADS, 2)), dma(())]
        + [dma((HEADS, 2))] * 8,
        compiler_params=pltpu.CompilerParams(
            collective_id=0, has_side_effects=True, vmem_limit_bytes=44 * 1024 * 1024
        ),
    )(*operands)
    results = [pltpu.with_memory_space_constraint(result, pltpu.VMEM) for result in results]
    return pl.pallas_call(
        store_kernel,
        out_shape=[jax.ShapeDtypeStruct(shape, bf16) for shape in shapes],
        in_specs=[vmem] * 4,
        out_specs=[pl.BlockSpec(memory_space=pltpu.HBM)] * 4,
        scratch_shapes=[dma((4, SPLIT))],
        compiler_params=pltpu.CompilerParams(vmem_limit_bytes=1024 * 1024),
    )(*results)


def solution(mesh):
    split = P(("outer", "inner"), None)
    return jax.shard_map(
        functools.partial(body, mesh.shape["outer"], mesh.shape["inner"]),
        mesh=mesh,
        in_specs=(split, split, split, split, P()),
        out_specs=(split, split, split, split),
        check_vma=False,
    )
```
